32 devices in a mesh: dp: 16 (over z, y, x), tm: 2 (over core).
Axes of the slice: x: 2, y: 2, z: 4, core: 2. Of those that a mesh axis runs over, the one named last changes fastest.
Arguments:
- mel: bfloat16 [16, 640, 640], P('dp', 'tm'), may hold values from -6 to 6
- cotangent: bfloat16 [16, 640, 1024], P('dp', 'tm'), may hold values from -6 to 6
- conv_one: bfloat16 [240, 256], replicated, may hold values from -0.375 to 0.375
- conv_two: bfloat16 [768, 256], replicated, may hold values from -0.21875 to 0.21875
- conv_three: bfloat16 [768, 256], replicated, may hold values from -0.21875 to 0.21875
- linear_weight: bfloat16 [256, 1024], replicated, may hold values from -0.375 to 0.375
- ln_gain: float32 [1024], replicated, may hold values from 0.5 to 1.5
- ln_bias: float32 [1024], replicated, may hold values from -3 to 3
- proj: bfloat16 [1024, 2048], P(None, 'tm'), may hold values from -0.1875 to 0.1875
- dw_kernel: bfloat16 [9, 1024], replicated, may hold values from -2 to 2
- blocks: int32 [16], replicated, may hold values from 1 to 16, as said below
Outputs:
- grad_conv_one: bfloat16 [240, 256], replicated
- grad_conv_two: bfloat16 [768, 256], replicated
- grad_conv_three: bfloat16 [768, 256], replicated
- grad_lin: bfloat16 [256, 1024], replicated
- grad_gain: bfloat16 [1024], replicated
- grad_bias: bfloat16 [1024], replicated
- grad_kernel: bfloat16 [9, 1024], replicated
The draws below stay inside these ranges and needn't reach their ends.
Inputs may be any that keep to these rules, and one draw needn't show every extreme that they name: blocks sum to 86 and the largest is exactly 16.
All inputs are finite; a program needn't handle non-finite values.
Results may differ from the reference program's by a relative error of at most 0.017.
Values may be sent and summed in bfloat16 or wider, within the bound.
No kernel may reach another device: no remote copies, remote signals or barrier semaphores. Data moves between devices by JAX's collectives and lax.ppermute only.
A program may use at most 64 MiB of HBM per device.

```python
import jax
import jax.numpy as jnp
from jax import lax

D = 1024
MELS = 80
SUBCH = 256
KERNEL = 9
S_DEV = 320
FOLD = 640
BLK_DEV = 16
BLK = 20
TOTAL_BLKS = 86
REC_ROWS = 640
ROWS_ALL = 3440
N_DP = 16
N_TM = 2


def draw_blocks(key, part):
    entries = BLK_DEV
    largest = BLK_DEV
    overall = TOTAL_BLKS
    pick_key, grid_key = jax.random.split(jax.random.fold_in(key, 17))
    planted = jax.random.randint(pick_key, (), 0, entries)
    remaining_items = entries - 1
    spare_units = overall - largest - remaining_items
    grid_cells = jax.random.permutation(grid_key, remaining_items * (largest - 1))
    chosen = grid_cells[:spare_units]
    row_lookup = chosen // (largest - 1)
    surplus_units = jnp.sum((row_lookup[None, :] == jnp.arange(remaining_items)[:, None]).astype(jnp.int32), axis=1)
    regular_rows = 1 + surplus_units
    indices = jnp.arange(entries)
    position = jnp.clip(indices - (indices > planted).astype(jnp.int32), 0, remaining_items - 1)
    values = jnp.where(indices == planted, largest, regular_rows[position])
    return values.astype(jnp.int32)


def shard_levels(rng, shape, cuts, least, high):
    def one(axis_at, parts):
        heights = jax.random.uniform(jax.random.fold_in(jax.random.fold_in(rng, 6), axis_at), (parts,), jnp.float32, least / len(cuts), high / len(cuts))
        return jnp.repeat(jnp.exp(heights), shape[axis_at] // parts).reshape((-1,) + (1,) * (len(shape) - axis_at - 1))

    gain = one(*cuts[0])
    for cut in cuts[1:]:
        gain = gain * one(*cut)
    return gain


def scatter_about(key, dims, width, reach, cuts=(), kind=jnp.bfloat16):
    level = shard_levels(key, dims, cuts, -0.22, 0.18) if cuts else 1.0
    values = jax.random.normal(key, dims, jnp.float32) * width * level
    return jnp.minimum(jnp.maximum(values, -reach), reach).astype(kind)


def setup_inputs(seed: int = 0) -> dict:
    streams_of = jax.random.split(jax.random.key(seed), 12)
    mel = scatter_about(streams_of[0], (N_DP, REC_ROWS, FOLD), 1.0, 6.0, ((0, 16), (1, 2)))
    cotangent = scatter_about(streams_of[1], (N_DP, REC_ROWS, D), 1.0, 6.0, ((0, 16), (1, 2)))
    conv_one = scatter_about(streams_of[2], (3 * MELS, SUBCH), (3 * MELS) ** -0.5, 0.375)
    conv_two = scatter_about(streams_of[3], (3 * SUBCH, SUBCH), (3 * SUBCH) ** -0.5, 0.21875)
    conv_three = scatter_about(streams_of[4], (3 * SUBCH, SUBCH), (3 * SUBCH) ** -0.5, 0.21875)
    linear_weight = scatter_about(streams_of[5], (SUBCH, D), SUBCH ** -0.5, 0.375)
    ln_gain = jnp.clip(1.0 + 0.1 * jax.random.normal(streams_of[6], (D,), jnp.float32), 0.5, 1.5)
    ln_bias = scatter_about(streams_of[7], (D,), 0.5, 3.0, (), jnp.float32)
    proj = scatter_about(streams_of[8], (D, 2 * D), D ** -0.5, 0.1875, ((1, 2),))
    dw_kernel = scatter_about(streams_of[9], (KERNEL, D), KERNEL ** -0.5, 2.0)
    blocks = draw_blocks(jax.random.fold_in(streams_of[11], 71), 0)
    return dict(mel=mel, cotangent=cotangent, conv_one=conv_one, conv_two=conv_two, conv_three=conv_three, linear_weight=linear_weight, ln_gain=ln_gain, ln_bias=ln_bias, proj=proj, dw_kernel=dw_kernel, blocks=blocks)


EPSILON = 1e-05

def product(lhs, rhs):
    return jnp.dot(lhs, rhs, preferred_element_type=jnp.float32)

def product_tn(lhs, rhs):
    return lax.dot_general(lhs, rhs, (((0,), (0,)), ((), ())), preferred_element_type=jnp.float32)

def product_nt(lhs, rhs):
    return lax.dot_general(lhs, rhs, (((1,), (1,)), ((), ())), preferred_element_type=jnp.float32)

def make_patches(values, starts):
    last_slot = values[:, -1, :]
    earlier = jnp.concatenate([jnp.zeros_like(last_slot[:1]), last_slot[:-1]], axis=0)
    earlier = earlier * (1 - starts).astype(values.dtype)[:, None]
    before_taps = jnp.concatenate([earlier[:, None, :], values[:, 1:-1:2, :]], axis=1)
    return jnp.concatenate([before_taps, values[:, 0::2, :], values[:, 1::2, :]], axis=2)

def silu_slope(pre_act):
    sigmoid_val = jax.nn.sigmoid(pre_act)
    return sigmoid_val * (1.0 + pre_act * (1.0 - sigmoid_val))

def subsample_forward(mel_rows, starts, conv_one, conv_two, conv_three, linear_weight):
    row_count = mel_rows.shape[0]
    current = mel_rows.reshape(row_count, 8, -1)
    stored = []
    for weight in (conv_one, conv_two, conv_three):
        patches = make_patches(current, starts)
        pre_act = product(patches.reshape(row_count * patches.shape[1], -1), weight)
        stored.append((patches, pre_act))
        current = jax.nn.silu(pre_act).astype(jnp.bfloat16).reshape(row_count, patches.shape[1], -1)
    top_section = current.reshape(row_count, -1)
    hidden = product(top_section, linear_weight).astype(jnp.bfloat16)
    return (hidden, top_section, stored)

def subsample_backward(grad_hidden, top_section, stored, starts, weights, linear_weight):
    row_count = top_section.shape[0]
    grad_lin = product_tn(top_section, grad_hidden)
    grad_act = product_nt(grad_hidden, linear_weight)
    conv_grads = [None, None, None]
    for section_index in (2, 1, 0):
        patches, pre_act = stored[section_index]
        grad_pre = (grad_act.reshape(pre_act.shape) * silu_slope(pre_act)).astype(jnp.bfloat16)
        conv_grads[section_index] = product_tn(patches.reshape(pre_act.shape[0], -1), grad_pre)
        if section_index > 0:
            grad_patch = product_nt(grad_pre, weights[section_index]).reshape(patches.shape)
            input_shape = (row_count, patches.shape[1] * 2, patches.shape[2] // 3)
            _, pullback = jax.vjp(lambda inner: make_patches(inner, starts), jnp.zeros(input_shape, jnp.float32))
            grad_act = pullback(grad_patch)[0]
    return (grad_lin, conv_grads)

def gated_forward(hidden, ln_gain, ln_bias, proj):
    values = hidden.astype(jnp.float32)
    centre = lax.optimization_barrier(jnp.mean(values, axis=-1, keepdims=True))
    spread = lax.optimization_barrier(jnp.mean(jnp.square(values - centre), axis=-1, keepdims=True))
    inverse_std = lax.rsqrt(spread + EPSILON)
    normed = (values - centre) * inverse_std
    shifted = (normed * ln_gain + ln_bias).astype(jnp.bfloat16)
    projected = product(shifted, proj)
    model_width = proj.shape[0]
    linear_part = projected[:, :model_width]
    sigmoid_gate = jax.nn.sigmoid(projected[:, model_width:])
    gated_rows = (linear_part * sigmoid_gate).astype(jnp.bfloat16)
    return (gated_rows, (normed, inverse_std, linear_part, sigmoid_gate))

def gated_backward(grad_gated, state, ln_gain, proj):
    normed, inverse_std, linear_part, sigmoid_gate = state
    upstream = grad_gated.astype(jnp.float32)
    grad_linear = upstream * sigmoid_gate
    grad_gate = upstream * linear_part * sigmoid_gate * (1.0 - sigmoid_gate)
    grad_projected = jnp.concatenate([grad_linear, grad_gate], axis=-1).astype(jnp.bfloat16)
    grad_shifted = product_nt(grad_projected, proj)
    grad_gain = lax.optimization_barrier(jnp.sum(grad_shifted * normed, axis=0))
    grad_bias = lax.optimization_barrier(jnp.sum(grad_shifted, axis=0))
    grad_normed = grad_shifted * ln_gain
    grad_values = inverse_std * (grad_normed - lax.optimization_barrier(jnp.mean(grad_normed, axis=-1, keepdims=True)) - normed * lax.optimization_barrier(jnp.mean(grad_normed * normed, axis=-1, keepdims=True)))
    return (grad_values.astype(jnp.bfloat16), grad_gain, grad_bias)

def reference(mel, cotangent, conv_one, conv_two, conv_three, linear_weight, ln_gain, ln_bias, proj, dw_kernel, blocks):
    share_rows = blocks * BLK
    record_len = share_rows * N_TM
    record_end = jnp.cumsum(record_len)
    record_start = record_end - record_len
    places = jnp.arange(ROWS_ALL, dtype=jnp.int32)
    record_of = lax.optimization_barrier(jnp.sum((record_end[None, :] <= places[:, None]).astype(jnp.int32), axis=1))
    within = places - record_start[record_of]
    row_share = share_rows[record_of]
    share_index = within // row_share
    local_row = within - share_index * row_share
    flat_row = share_index * S_DEV + local_row
    mel_rows = mel[record_of, flat_row]
    cot_rows = cotangent[record_of, flat_row]
    starts = (within == 0).astype(jnp.int32)
    hidden, top_section, stored = subsample_forward(mel_rows, starts, conv_one, conv_two, conv_three, linear_weight)
    gated_rows, state = gated_forward(hidden, ln_gain, ln_bias, proj)
    loss_scale = lax.rsqrt(jnp.float32(ROWS_ALL))
    grad_out = cot_rows.astype(jnp.float32) * loss_scale
    length_row = record_len[record_of]
    half_width = KERNEL // 2
    padded = jnp.pad(gated_rows.astype(jnp.float32), ((half_width, half_width), (0, 0)))
    grad_pad = jnp.zeros_like(padded)
    kernel_terms = []
    for tap_index in range(KERNEL):
        target = within + tap_index - half_width
        inside = ((target >= 0) & (target < length_row)).astype(jnp.float32)[:, None]
        weighted = grad_out * inside
        kernel_terms.append(lax.optimization_barrier(jnp.sum(weighted * padded[tap_index:tap_index + ROWS_ALL], axis=0)))
        grad_pad = grad_pad.at[tap_index:tap_index + ROWS_ALL].add(weighted * dw_kernel[tap_index].astype(jnp.float32))
    grad_gated = grad_pad[half_width:half_width + ROWS_ALL].astype(jnp.bfloat16)
    grad_hidden, grad_gain, grad_bias = gated_backward(grad_gated, state, ln_gain, proj)
    grad_lin, conv_grads = subsample_backward(grad_hidden, top_section, stored, starts, (conv_one, conv_two, conv_three), linear_weight)
    grad_kernel = jnp.stack(kernel_terms, axis=0)
    return (conv_grads[0].astype(jnp.bfloat16), conv_grads[1].astype(jnp.bfloat16), conv_grads[2].astype(jnp.bfloat16), grad_lin.astype(jnp.bfloat16), grad_gain.astype(jnp.bfloat16), grad_bias.astype(jnp.bfloat16), grad_kernel.astype(jnp.bfloat16))
```

```python
import jax
import jax.numpy as jnp
from jax import lax
from jax.sharding import PartitionSpec as P

EPSILON = 1e-05
BF16 = jnp.bfloat16
F32 = jnp.float32
PAD = 16
LANES = 256


def dot(lhs, rhs):
    return lax.dot_general(lhs, rhs, (((1,), (0,)), ((), ())), preferred_element_type=F32)


def dot_tn(lhs, rhs):
    return lax.dot_general(lhs, rhs, (((0,), (0,)), ((), ())), preferred_element_type=F32)


def dot_nt(lhs, rhs):
    return lax.dot_general(lhs, rhs, (((1,), (1,)), ((), ())), preferred_element_type=F32)


def down(rows):
    return jnp.concatenate([rows[-1:], rows[:-1]], axis=0)


def up(rows):
    return jnp.concatenate([rows[1:], rows[:1]], axis=0)


def silu_and_slope(z):
    sig = jax.nn.sigmoid(z)
    return (z * sig).astype(BF16), sig * (1.0 + z * (1.0 - sig))


def band_weight(conv_one, fold):
    mels = conv_one.shape[0] // 3
    columns = []
    for j in range(4):
        first = (2 * j - 1) * mels
        if j == 0:
            body = conv_one[mels:]
            first = 0
        else:
            body = conv_one
        columns.append(jnp.pad(body, ((first, fold - first - body.shape[0]), (0, 0))))
    return jnp.concatenate(columns, axis=1)


def partner(axis, bit):
    count = lax.axis_size(axis)
    return [(i, i ^ (1 << bit)) for i in range(count)]


def bit_of(axis, bit):
    return (lax.axis_index(axis) >> bit) & 1


def halve(rows, axis, bit):
    half = rows.shape[0] // 2
    mine = bit_of(axis, bit)
    sent = lax.dynamic_slice_in_dim(rows, (1 - mine) * half, half, 0)
    kept = lax.dynamic_slice_in_dim(rows, mine * half, half, 0)
    got = lax.ppermute(sent, axis, partner(axis, bit))
    return (kept.astype(F32) + got.astype(F32)).astype(BF16)


def double(rows, axis, bit):
    got = lax.ppermute(rows, axis, partner(axis, bit))
    return (rows.astype(F32) + got.astype(F32)).astype(BF16)


def join(rows, axis, bit):
    got = lax.ppermute(rows, axis, partner(axis, bit))
    first = bit_of(axis, bit) == 0
    return jnp.concatenate([jnp.where(first, rows, got), jnp.where(first, got, rows)], axis=0)


def chain(rows, stages, last):
    for axis, bit in stages:
        rows = halve(rows, axis, bit)
    rows = double(rows, *last)
    for axis, bit in reversed(stages):
        rows = join(rows, axis, bit)
    return rows


def total_sum(rows):
    dp_bits = lax.axis_size("dp").bit_length() - 1
    tm_bits = lax.axis_size("tm").bit_length() - 1
    near = [("tm", b) for b in range(tm_bits)]
    for stage in near:
        rows = halve(rows, *stage)
    far = [("dp", b) for b in range(dp_bits - 1)]
    last = ("dp", dp_bits - 1)
    half = rows.shape[0] // 2
    one = chain(rows[:half], far, last)
    swapped = [far[1], far[0]] + far[2:]
    two = chain(rows[half:], swapped, last)
    rows = jnp.concatenate([one, two], axis=0)
    for stage in reversed(near):
        rows = join(rows, *stage)
    return rows


def per_device(
    mel,
    cotangent,
    conv_one,
    conv_two,
    conv_three,
    linear_weight,
    ln_gain,
    ln_bias,
    proj,
    dw_kernel,
    blocks,
):
    dp_count = lax.axis_size("dp")
    tm_count = lax.axis_size("tm")
    dp_rank = lax.axis_index("dp")
    mel = mel[0]
    cot = cotangent[0]
    rows_dev, fold = mel.shape
    mels = conv_one.shape[0] // 3
    sub = conv_one.shape[1]
    width = linear_weight.shape[1]
    taps = dw_kernel.shape[0]
    half = taps // 2
    block_rows = rows_dev // dp_count
    total_blocks = (dp_count * dp_count + 2) // 3
    live_rows = blocks[dp_rank] * block_rows
    scale = lax.rsqrt(jnp.float32(total_blocks * block_rows * tm_count))
    to_right = [(i, i + 1) for i in range(tm_count - 1)]
    to_left = [(i + 1, i) for i in range(tm_count - 1)]

    rest = [proj]
    for k in range(1, tm_count):
        rest.append(lax.ppermute(proj, "tm", [(i, (i + k) % tm_count) for i in range(tm_count)]))
    pieces = jnp.stack(rest)
    order = jnp.mod(lax.axis_index("tm") - jnp.arange(tm_count), tm_count)
    proj_full = jnp.concatenate([pieces[order[j]] for j in range(tm_count)], axis=1)

    last_mel = lax.dynamic_slice_in_dim(mel, live_rows - 1, 1, 0)
    last_cot = lax.dynamic_slice_in_dim(cot, live_rows - half, half, 0)
    context = lax.ppermute(last_mel, "tm", to_right)
    cot_left = lax.ppermute(last_cot, "tm", to_right)
    cot_right = lax.ppermute(cot[:half], "tm", to_left)

    mel_ext = jnp.concatenate([mel, jnp.zeros((PAD - 1, fold), BF16), context], axis=0)
    rows_ext = rows_dev + PAD
    live = jnp.arange(rows_ext)[:, None] < live_rows

    z1 = dot(mel_ext, band_weight(conv_one, fold))
    back = down(dot(mel_ext[:, fold - mels :], conv_one[:mels]))
    z1 = jnp.concatenate([z1[:, :sub] + back, z1[:, sub:]], axis=1)
    a1, slope1 = silu_and_slope(z1)
    z2 = jnp.concatenate(
        [
            dot(a1[:, : 2 * sub], conv_two[sub:]) + down(dot(a1[:, 3 * sub :], conv_two[:sub])),
            dot(a1[:, sub:], conv_two),
        ],
        axis=1,
    )
    a2, slope2 = silu_and_slope(z2)
    z3 = dot(a2, conv_three[sub:]) + down(dot(a2[:, sub:], conv_three[:sub]))
    a3, slope3 = silu_and_slope(z3)
    hidden = dot(a3, linear_weight).astype(BF16).astype(F32)
    centred = hidden - jnp.mean(hidden, axis=1, keepdims=True)
    inverse = lax.rsqrt(jnp.mean(centred * centred, axis=1, keepdims=True) + EPSILON)
    normed = centred * inverse
    shifted = (normed * ln_gain + ln_bias).astype(BF16)
    projected = dot(shifted, proj_full)
    value, gate = projected[:, :width], projected[:, width:]
    sig = jax.nn.sigmoid(gate)
    gated = jnp.where(live, (value * sig).astype(BF16).astype(F32), 0.0)

    cot_ext = jnp.where(live[:rows_dev], cot.astype(F32), 0.0)
    cot_ext = jnp.concatenate([cot_left.astype(F32), cot_ext, jnp.zeros((PAD + half, width), F32)])
    cot_ext = lax.dynamic_update_slice_in_dim(
        cot_ext, cot_right.astype(F32), live_rows + half, 0
    )
    cot_ext = jnp.pad(cot_ext, ((0, half), (0, 0))) * scale
    grad_kernel = []
    eg = jnp.zeros((rows_ext, width), F32)
    for k in range(taps):
        view = cot_ext[2 * half - k : 2 * half - k + rows_ext]
        grad_kernel.append(jnp.sum(gated * view, axis=0))
        eg = eg + dw_kernel[k].astype(F32) * view
    eg = jnp.where(live, eg, 0.0).astype(BF16).astype(F32)
    em = jnp.concatenate([eg * sig, eg * value * sig * (1.0 - sig)], axis=1).astype(BF16)
    du = dot_nt(em, proj_full)
    grad_gain = jnp.sum(du * normed, axis=0)
    grad_bias = jnp.sum(du, axis=0)
    e = du * ln_gain
    dh = inverse * (
        e
        - jnp.mean(e, axis=1, keepdims=True)
        - normed * jnp.mean(e * normed, axis=1, keepdims=True)
    )
    dh = dh.astype(BF16)
    grad_lin = dot_tn(a3, dh)
    ez3 = dot_nt(dh, linear_weight) * slope3
    ez3_up = up(ez3).astype(BF16)
    ez3 = ez3.astype(BF16)
    grad_three = jnp.concatenate([dot_tn(a2[:, sub:], ez3_up), dot_tn(a2, ez3)], axis=0)
    da2 = dot_nt(ez3, conv_three[sub:])
    da2 = jnp.concatenate(
        [da2[:, :sub], da2[:, sub:] + dot_nt(ez3_up, conv_three[:sub])], axis=1
    )
    ez2 = da2 * slope2
    ez2_up = up(ez2[:, :sub]).astype(BF16)
    ez2 = ez2.astype(BF16)
    first, second = ez2[:, :sub], ez2[:, sub:]
    second_grad = dot_tn(a1[:, sub:], second)
    grad_two = second_grad + jnp.concatenate(
        [dot_tn(a1[:, 3 * sub :], ez2_up), dot_tn(a1[:, : 2 * sub], first)], axis=0
    )
    from_first = dot_nt(first, conv_two[sub:])
    from_second = dot_nt(second, conv_two)
    da1 = jnp.concatenate(
        [
            from_first[:, :sub],
            from_first[:, sub:] + from_second[:, :sub],
            from_second[:, sub : 2 * sub],
            from_second[:, 2 * sub :] + dot_nt(ez2_up, conv_two[:sub]),
        ],
        axis=1,
    )
    ez1 = da1 * slope1
    ez1_up = up(ez1[:, :sub]).astype(BF16)
    ez1 = ez1.astype(BF16)
    wide = dot_tn(mel_ext, ez1)
    grad_one = jnp.concatenate(
        [dot_tn(mel_ext[:, fold - mels :], ez1_up), wide[: 2 * mels, :sub]], axis=0
    )
    for j in range(1, 4):
        start = (2 * j - 1) * mels
        grad_one = grad_one + wide[start : start + 3 * mels, j * sub : (j + 1) * sub]

    small = jnp.concatenate([grad_gain[None], grad_bias[None], jnp.stack(grad_kernel)], axis=0)
    small = jnp.pad(small, ((0, 16 - small.shape[0]), (0, 0)))
    parts = [grad_lin, small, grad_three, grad_two, grad_one]
    flat = []
    for part in parts:
        flat.extend(part[:, c : c + LANES] for c in range(0, part.shape[1], LANES))
    flat = jnp.concatenate(flat, axis=0).astype(BF16)
    unit = 2 * dp_count * tm_count
    size = -(-flat.shape[0] // unit) * unit
    summed = total_sum(jnp.pad(flat, ((0, size - flat.shape[0]), (0, 0))))
    results = []
    offset = 0
    for part in parts:
        rows, columns = part.shape
        results.append(
            jnp.concatenate(
                [
                    summed[offset + c * rows : offset + (c + 1) * rows]
                    for c in range(columns // LANES)
                ],
                axis=1,
            )
        )
        offset += rows * (columns // LANES)
    out_lin, out_small, out_three, out_two, out_one = results
    return (
        out_one,
        out_two,
        out_three,
        out_lin,
        out_small[0],
        out_small[1],
        out_small[2 : 2 + taps],
    )


def solution(mesh):
    return jax.shard_map(
        per_device,
        mesh=mesh,
        in_specs=(
            P("dp", "tm", None),
            P("dp", "tm", None),
            P(),
            P(),
            P(),
            P(),
            P(),
            P(),
            P(None, "tm"),
            P(),
            P(),
        ),
        out_specs=(P(), P(), P(), P(), P(), P(), P()),
        check_vma=False,
    )
```

```python
import jax
import jax.numpy as jnp
from jax import lax
from jax.sharding import PartitionSpec as P

EPSILON = 1e-05
BF16 = jnp.bfloat16
F32 = jnp.float32
PAD = 16
LANES = 256


def dot(lhs, rhs):
    return lax.dot_general(lhs, rhs, (((1,), (0,)), ((), ())), preferred_element_type=F32)


def dot_tn(lhs, rhs):
    return lax.dot_general(lhs, rhs, (((0,), (0,)), ((), ())), preferred_element_type=F32)


def dot_nt(lhs, rhs):
    return lax.dot_general(lhs, rhs, (((1,), (1,)), ((), ())), preferred_element_type=F32)


def down(rows):
    return jnp.concatenate([rows[-1:], rows[:-1]], axis=0)


def up(rows):
    return jnp.concatenate([rows[1:], rows[:1]], axis=0)


def silu_and_slope(z):
    sig = jax.nn.sigmoid(z)
    return (z * sig).astype(BF16), sig * (1.0 + z * (1.0 - sig))


def band_weight(conv_one, fold):
    mels = conv_one.shape[0] // 3
    columns = []
    for j in range(4):
        first = (2 * j - 1) * mels
        if j == 0:
            body = conv_one[mels:]
            first = 0
        else:
            body = conv_one
        columns.append(jnp.pad(body, ((first, fold - first - body.shape[0]), (0, 0))))
    return jnp.concatenate(columns, axis=1)


def partner(stage):
    axis, bits = stage
    count = lax.axis_size(axis)
    if axis == "tm":
        return "tm", [(i, i ^ (1 << bits[0])) for i in range(count)]
    shares = lax.axis_size("tm")
    pairs = []
    for i in range(count):
        for j in range(shares):
            pairs.append((i * shares + j, (i ^ (1 << bits[j % 2])) * shares + j))
    return ("dp", "tm"), pairs


def side_of(stage):
    axis, bits = stage
    rank = lax.axis_index(axis)
    if axis == "tm":
        return (rank >> bits[0]) & 1
    odd = lax.axis_index("tm") % 2
    return jnp.where(odd == 1, rank >> bits[1], rank >> bits[0]) & 1


def swap(rows, stage):
    axes, pairs = partner(stage)
    return lax.ppermute(rows, axes, pairs)


def halve(rows, stage):
    half = rows.shape[0] // 2
    mine = side_of(stage)
    sent = lax.dynamic_slice_in_dim(rows, (1 - mine) * half, half, 0)
    kept = lax.dynamic_slice_in_dim(rows, mine * half, half, 0)
    return (kept.astype(F32) + swap(sent, stage).astype(F32)).astype(BF16)


def double(rows, stage):
    return (rows.astype(F32) + swap(rows, stage).astype(F32)).astype(BF16)


def join(rows, stage):
    got = swap(rows, stage)
    first = side_of(stage) == 0
    return jnp.concatenate([jnp.where(first, rows, got), jnp.where(first, got, rows)], axis=0)


def total_sum(rows):
    dp_bits = lax.axis_size("dp").bit_length() - 1
    tm_bits = lax.axis_size("tm").bit_length() - 1
    stages = [("tm", (b,)) for b in range(tm_bits)]
    inner = dp_bits - 1
    stages += [("dp", (b, (b + 1) % inner)) for b in range(inner)]
    for stage in stages:
        rows = halve(rows, stage)
    rows = double(rows, ("dp", (inner, inner)))
    for stage in reversed(stages):
        rows = join(rows, stage)
    return rows


def per_device(
    mel,
    cotangent,
    conv_one,
    conv_two,
    conv_three,
    linear_weight,
    ln_gain,
    ln_bias,
    proj,
    dw_kernel,
    blocks,
):
    dp_count = lax.axis_size("dp")
    tm_count = lax.axis_size("tm")
    dp_rank = lax.axis_index("dp")
    mel = mel[0]
    cot = cotangent[0]
    rows_dev, fold = mel.shape
    mels = conv_one.shape[0] // 3
    sub = conv_one.shape[1]
    width = linear_weight.shape[1]
    taps = dw_kernel.shape[0]
    half = taps // 2
    block_rows = rows_dev // dp_count
    total_blocks = (dp_count * dp_count + 2) // 3
    live_rows = blocks[dp_rank] * block_rows
    scale = lax.rsqrt(jnp.float32(total_blocks * block_rows * tm_count))
    to_right = [(i, i + 1) for i in range(tm_count - 1)]
    to_left = [(i + 1, i) for i in range(tm_count - 1)]

    rest = [proj]
    for k in range(1, tm_count):
        rest.append(lax.ppermute(proj, "tm", [(i, (i + k) % tm_count) for i in range(tm_count)]))
    pieces = jnp.stack(rest)
    order = jnp.mod(lax.axis_index("tm") - jnp.arange(tm_count), tm_count)
    proj_full = jnp.concatenate([pieces[order[j]] for j in range(tm_count)], axis=1)

    last_mel = lax.dynamic_slice_in_dim(mel, live_rows - 1, 1, 0)
    last_cot = lax.dynamic_slice_in_dim(cot, live_rows - half, half, 0)
    context = lax.ppermute(last_mel, "tm", to_right)
    cot_left = lax.ppermute(last_cot, "tm", to_right)
    cot_right = lax.ppermute(cot[:half], "tm", to_left)

    mel_ext = jnp.concatenate([mel, jnp.zeros((PAD - 1, fold), BF16), context], axis=0)
    rows_ext = rows_dev + PAD
    live = jnp.arange(rows_ext)[:, None] < live_rows

    z1 = dot(mel_ext, band_weight(conv_one, fold))
    back = down(dot(mel_ext[:, fold - mels :], conv_one[:mels]))
    z1 = jnp.concatenate([z1[:, :sub] + back, z1[:, sub:]], axis=1)
    a1, slope1 = silu_and_slope(z1)
    z2 = jnp.concatenate(
        [
            dot(a1[:, : 2 * sub], conv_two[sub:]) + down(dot(a1[:, 3 * sub :], conv_two[:sub])),
            dot(a1[:, sub:], conv_two),
        ],
        axis=1,
    )
    a2, slope2 = silu_and_slope(z2)
    z3 = dot(a2, conv_three[sub:]) + down(dot(a2[:, sub:], conv_three[:sub]))
    a3, slope3 = silu_and_slope(z3)
    hidden = dot(a3, linear_weight).astype(BF16).astype(F32)
    centred = hidden - jnp.mean(hidden, axis=1, keepdims=True)
    inverse = lax.rsqrt(jnp.mean(centred * centred, axis=1, keepdims=True) + EPSILON)
    normed = centred * inverse
    shifted = (normed * ln_gain + ln_bias).astype(BF16)
    projected = dot(shifted, proj_full)
    value, gate = projected[:, :width], projected[:, width:]
    sig = jax.nn.sigmoid(gate)
    gated = jnp.where(live, (value * sig).astype(BF16).astype(F32), 0.0)

    cot_ext = jnp.where(live[:rows_dev], cot.astype(F32), 0.0)
    cot_ext = jnp.concatenate([cot_left.astype(F32), cot_ext, jnp.zeros((PAD + half, width), F32)])
    cot_ext = lax.dynamic_update_slice_in_dim(
        cot_ext, cot_right.astype(F32), live_rows + half, 0
    )
    cot_ext = jnp.pad(cot_ext, ((0, half), (0, 0))) * scale
    grad_kernel = []
    eg = jnp.zeros((rows_ext, width), F32)
    for k in range(taps):
        view = cot_ext[2 * half - k : 2 * half - k + rows_ext]
        grad_kernel.append(jnp.sum(gated * view, axis=0))
        eg = eg + dw_kernel[k].astype(F32) * view
    eg = jnp.where(live, eg, 0.0).astype(BF16).astype(F32)
    em = jnp.concatenate([eg * sig, eg * value * sig * (1.0 - sig)], axis=1).astype(BF16)
    du = dot_nt(em, proj_full)
    grad_gain = jnp.sum(du * normed, axis=0)
    grad_bias = jnp.sum(du, axis=0)
    e = du * ln_gain
    dh = inverse * (
        e
        - jnp.mean(e, axis=1, keepdims=True)
        - normed * jnp.mean(e * normed, axis=1, keepdims=True)
    )
    dh = dh.astype(BF16)
    grad_lin = dot_tn(a3, dh)
    ez3 = dot_nt(dh, linear_weight) * slope3
    ez3_up = up(ez3).astype(BF16)
    ez3 = ez3.astype(BF16)
    grad_three = jnp.concatenate([dot_tn(a2[:, sub:], ez3_up), dot_tn(a2, ez3)], axis=0)
    da2 = dot_nt(ez3, conv_three[sub:])
    da2 = jnp.concatenate(
        [da2[:, :sub], da2[:, sub:] + dot_nt(ez3_up, conv_three[:sub])], axis=1
    )
    ez2 = da2 * slope2
    ez2_up = up(ez2[:, :sub]).astype(BF16)
    ez2 = ez2.astype(BF16)
    first, second = ez2[:, :sub], ez2[:, sub:]
    second_grad = dot_tn(a1[:, sub:], second)
    grad_two = second_grad + jnp.concatenate(
        [dot_tn(a1[:, 3 * sub :], ez2_up), dot_tn(a1[:, : 2 * sub], first)], axis=0
    )
    from_first = dot_nt(first, conv_two[sub:])
    from_second = dot_nt(second, conv_two)
    da1 = jnp.concatenate(
        [
            from_first[:, :sub],
            from_first[:, sub:] + from_second[:, :sub],
            from_second[:, sub : 2 * sub],
            from_second[:, 2 * sub :] + dot_nt(ez2_up, conv_two[:sub]),
        ],
        axis=1,
    )
    ez1 = da1 * slope1
    ez1_up = up(ez1[:, :sub]).astype(BF16)
    ez1 = ez1.astype(BF16)
    wide = dot_tn(mel_ext, ez1)
    grad_one = jnp.concatenate(
        [dot_tn(mel_ext[:, fold - mels :], ez1_up), wide[: 2 * mels, :sub]], axis=0
    )
    for j in range(1, 4):
        start = (2 * j - 1) * mels
        grad_one = grad_one + wide[start : start + 3 * mels, j * sub : (j + 1) * sub]

    small = jnp.concatenate([grad_gain[None], grad_bias[None], jnp.stack(grad_kernel)], axis=0)
    small = jnp.pad(small, ((0, 16 - small.shape[0]), (0, 0)))
    parts = [grad_lin, small, grad_three, grad_two, grad_one]
    flat = []
    for part in parts:
        flat.extend(part[:, c : c + LANES] for c in range(0, part.shape[1], LANES))
    flat = jnp.concatenate(flat, axis=0).astype(BF16)
    unit = 8 * (dp_count * tm_count // 2)
    size = -(-flat.shape[0] // unit) * unit
    summed = total_sum(jnp.pad(flat, ((0, size - flat.shape[0]), (0, 0))))
    results = []
    offset = 0
    for part in parts:
        rows, columns = part.shape
        results.append(
            jnp.concatenate(
                [
                    summed[offset + c * rows : offset + (c + 1) * rows]
                    for c in range(columns // LANES)
                ],
                axis=1,
            )
        )
        offset += rows * (columns // LANES)
    out_lin, out_small, out_three, out_two, out_one = results
    return (
        out_one,
        out_two,
        out_three,
        out_lin,
        out_small[0],
        out_small[1],
        out_small[2 : 2 + taps],
    )


def solution(mesh):
    return jax.shard_map(
        per_device,
        mesh=mesh,
        in_specs=(
            P("dp", "tm", None),
            P("dp", "tm", None),
            P(),
            P(),
            P(),
            P(),
            P(),
            P(),
            P(None, "tm"),
            P(),
            P(),
        ),
        out_specs=(P(), P(), P(), P(), P(), P(), P()),
        check_vma=False,
    )
```

```python
import functools
import math

import jax
import jax.numpy as jnp
from jax import lax
from jax.experimental import pallas as pl
from jax.experimental.pallas import tpu as pltpu
from jax.sharding import PartitionSpec as P

EPSILON = 1e-05
BF16 = jnp.bfloat16
F32 = jnp.float32
PAD = 16
LANES = 256
HALF = 4
GROUPS = 14
VMEM_BYTES = 48 << 20


def dot(lhs, rhs):
    return lax.dot_general(lhs, rhs, (((1,), (0,)), ((), ())), preferred_element_type=F32)


def dot_tn(lhs, rhs):
    return lax.dot_general(lhs, rhs, (((0,), (0,)), ((), ())), preferred_element_type=F32)


def dot_nt(lhs, rhs):
    return lax.dot_general(lhs, rhs, (((1,), (1,)), ((), ())), preferred_element_type=F32)


def down(rows):
    count = rows.shape[0]
    return jnp.concatenate([pltpu.roll(rows[count - 8 :], 1, 0), rows[: count - 8]], axis=0)


def up(rows):
    return jnp.concatenate([rows[8:], pltpu.roll(rows[:8], 7, 0)], axis=0)


def frame_of(shape, first, stride):
    place = lax.broadcasted_iota(jnp.int32, shape, 0)
    return (place & 7) * stride + (place >> 3) + first


def act(z):
    sig = 1.0 / (1.0 + jnp.exp(-z))
    return (z * sig).astype(BF16), (sig * (1.0 + z * (1.0 - sig))).astype(BF16)


def activate(z_ref, a_ref, slope_ref):
    rows, columns = z_ref.shape

    def step(i, carry):
        here = pl.ds(pl.multiple_of(i * 16, 16), 16)
        a, slope = act(z_ref[here, :])
        a_ref[here, :] = a
        slope_ref[here, :] = slope
        return carry

    lax.fori_loop(0, rows // 16, step, 0)


def front(
    live_ref,
    mel_ref,
    cot_ref,
    halo_ref,
    one_ref,
    two_ref,
    three_ref,
    lin_ref,
    gain_ref,
    bias_ref,
    mel_out,
    cot_out,
    a1_ref,
    slope1_ref,
    a2_ref,
    slope2_ref,
    a3_ref,
    slope3_ref,
    hidden_ref,
    shifted_ref,
    band,
    wide,
    source,
):
    rows_dev, fold = mel_ref.shape
    rows = mel_out.shape[0]
    stride = rows // 8
    width = cot_ref.shape[1]
    mels = one_ref.shape[0] // 3
    sub = one_ref.shape[1]
    live = live_ref[0]

    shape = (rows, rows_dev)
    frame = frame_of(shape, 0, stride)
    pick = (frame == lax.broadcasted_iota(jnp.int32, shape, 1)).astype(BF16)
    shape = (rows, 16)
    column = lax.broadcasted_iota(jnp.int32, shape, 1)
    extra = ((frame_of(shape, 0, stride) == rows - 1) & (column == 15)).astype(BF16)
    mel_out[...] = (dot(pick, mel_ref[...]) + dot(extra, halo_ref[:, width:])).astype(BF16)

    shape = (cot_out.shape[0], rows_dev)
    frame = frame_of(shape, -HALF, stride)
    column = lax.broadcasted_iota(jnp.int32, shape, 1)
    pick = ((frame == column) & (column < live)).astype(BF16)
    shape = (cot_out.shape[0], 16)
    frame = frame_of(shape, -HALF, stride)
    column = lax.broadcasted_iota(jnp.int32, shape, 1)
    before = (column >= 12) & (frame == column - 16)
    after = (column < HALF) & (frame == column + live)
    cot_out[...] = (
        dot(pick, cot_ref[...]) + dot((before | after).astype(BF16), halo_ref[:, :width])
    ).astype(BF16)

    band[...] = jnp.zeros_like(band)
    band[: 2 * mels, :sub] = one_ref[mels:, :]
    for j in range(1, 4):
        first = (2 * j - 1) * mels
        band[first : first + 3 * mels, j * sub : (j + 1) * sub] = one_ref[...]
    wide[...] = dot(mel_out[...], band[...])
    source[...] = jnp.zeros_like(source)
    source[128 - mels :, :] = one_ref[:mels, :]
    wide[:, :sub] += down(dot(mel_out[:, fold - 128 :], source[...]))
    activate(wide, a1_ref, slope1_ref)

    z2 = wide.at[:, : 2 * sub]
    z2[:, :sub] = dot(a1_ref[:, : 2 * sub], two_ref[sub:, :]) + down(
        dot(a1_ref[:, 3 * sub :], two_ref[:sub, :])
    )
    z2[:, sub:] = dot(a1_ref[:, sub:], two_ref[...])
    activate(z2, a2_ref, slope2_ref)

    z3 = wide.at[:, :sub]
    z3[...] = dot(a2_ref[...], three_ref[sub:, :]) + down(dot(a2_ref[:, sub:], three_ref[:sub, :]))
    activate(z3, a3_ref, slope3_ref)

    hidden_ref[...] = dot(a3_ref[...], lin_ref[...]).astype(BF16)

    def norm(i, carry):
        here = pl.ds(pl.multiple_of(i * 16, 16), 16)
        normed, _ = normal(hidden_ref[here, :])
        shifted_ref[here, :] = (normed * gain_ref[...] + bias_ref[...]).astype(BF16)
        return carry

    lax.fori_loop(0, rows // 16, norm, 0)


def normal(hidden):
    values = hidden.astype(F32)
    centred = values - jnp.mean(values, axis=1, keepdims=True)
    inverse = lax.rsqrt(jnp.mean(centred * centred, axis=1, keepdims=True) + EPSILON)
    return centred * inverse, inverse


def middle(
    live_ref,
    shifted_ref,
    hidden_ref,
    cot_ref,
    proj_ref,
    tap_ref,
    gain_ref,
    lin_ref,
    three_ref,
    a3_ref,
    slope3_ref,
    a2_ref,
    slope2_ref,
    lin_out,
    three_out,
    small_out,
    ez2_ref,
    ez2_up_ref,
    value,
    gate,
    em,
    dh,
    sums,
    *,
    scale,
):
    rows, width = hidden_ref.shape
    stride = rows // 8
    sub = lin_ref.shape[0]
    taps = tap_ref.shape[0]
    live = live_ref[0]
    pieces, _, piece = proj_ref.shape
    for j in range(pieces):
        at = j * piece
        target = value if at < width else gate
        at = at % width
        target[:, at : at + piece] = dot(shifted_ref[...], proj_ref[j])

    groups = GROUPS
    span = 8 * groups

    def tap_step(t, carry):
        here = pl.ds(pl.multiple_of(t * 128, 128), 128)
        there = pl.ds(pl.multiple_of(width + t * 128, 128), 128)
        sums_k = [jnp.zeros((8, 128), F32) for _ in range(taps)]
        weights = [tap_ref[k : k + 1, here].astype(F32) * scale for k in range(taps)]
        for c in range(rows // span):
            at = c * span
            window = cot_ref[at : at + span + 8 * (taps - 1), here].astype(F32)
            val = value[at : at + span, here]
            sig = 1.0 / (1.0 + jnp.exp(-gate[at : at + span, here]))
            alive = frame_of((span, 128), c * groups, stride) < live
            gated = jnp.where(alive, (val * sig).astype(BF16).astype(F32), 0.0)
            eg = jnp.zeros((span, 128), F32)
            for k in range(taps):
                first = 8 * (taps - 1 - k)
                view = window[first : first + span]
                eg = eg + weights[k] * view
                part = gated * view
                for g in range(groups):
                    sums_k[k] = sums_k[k] + part[8 * g : 8 * g + 8]
            eg = jnp.where(alive, eg, 0.0).astype(BF16).astype(F32)
            top = eg * sig
            em[at : at + span, here] = top.astype(BF16)
            em[at : at + span, there] = (top * val * (1.0 - sig)).astype(BF16)
        for k in range(taps):
            sums[k + 2 : k + 3, here] = jnp.sum(sums_k[k], axis=0, keepdims=True) * scale
        return carry

    sums[...] = jnp.zeros_like(sums)
    lax.fori_loop(0, width // 128, tap_step, 0)

    du = value
    total = dot_nt(em[:, :piece], proj_ref[0])
    for j in range(1, pieces):
        total = total + dot_nt(em[:, j * piece : (j + 1) * piece], proj_ref[j])
    du[...] = total

    def norm_back(i, carry):
        gain_sum, bias_sum = carry
        here = pl.ds(pl.multiple_of(i * 16, 16), 16)
        normed, inverse = normal(hidden_ref[here, :])
        grad = du[here, :]
        product = grad * normed
        gain_sum = gain_sum + product[:8] + product[8:]
        bias_sum = bias_sum + grad[:8] + grad[8:]
        e = grad * gain_ref[...]
        mean = jnp.mean(e, axis=1, keepdims=True)
        slant = jnp.mean(e * normed, axis=1, keepdims=True)
        dh[here, :] = (inverse * (e - mean - normed * slant)).astype(BF16)
        return gain_sum, bias_sum

    zero = jnp.zeros((8, width), F32)
    gain_sum, bias_sum = lax.fori_loop(0, rows // 16, norm_back, (zero, zero))
    sums[0:1, :] = jnp.sum(gain_sum, axis=0, keepdims=True)
    sums[1:2, :] = jnp.sum(bias_sum, axis=0, keepdims=True)
    for c in range(width // LANES):
        at = c * LANES
        small_out[c * 16 : c * 16 + 16, :] = sums[:, at : at + LANES].astype(BF16)
        lin_out[c * sub : (c + 1) * sub, :] = dot_tn(a3_ref[...], dh[:, at : at + LANES]).astype(
            BF16
        )

    ez3 = dot_nt(dh[...], lin_ref[...]) * slope3_ref[...].astype(F32)
    ez3_up = up(ez3).astype(BF16)
    ez3 = ez3.astype(BF16)
    three_out[:sub, :] = dot_tn(a2_ref[:, sub:], ez3_up).astype(BF16)
    three_out[sub:, :] = dot_tn(a2_ref[...], ez3).astype(BF16)
    da2 = dot_nt(ez3, three_ref[sub:, :])
    ez2 = da2[:, :sub] * slope2_ref[:, :sub].astype(F32)
    ez2_up_ref[...] = up(ez2).astype(BF16)
    ez2_ref[:, :sub] = ez2.astype(BF16)
    rest = da2[:, sub:] + dot_nt(ez3_up, three_ref[:sub, :])
    ez2_ref[:, sub:] = (rest * slope2_ref[:, sub:].astype(F32)).astype(BF16)


def rear(
    mel_ref, a1_ref, slope1_ref, ez2_ref, ez2_up_ref, two_ref, two_out, one_out, ez1, ez1_up, wide
):
    sub = two_ref.shape[1]
    fold = mel_ref.shape[1]
    mels = one_out.shape[0] // 3
    first, second = ez2_ref[:, :sub], ez2_ref[:, sub:]
    from_first = dot_nt(first, two_ref[sub:, :])
    from_second = dot_nt(second, two_ref[...])
    rows = from_first[:, :sub] * slope1_ref[:, :sub].astype(F32)
    ez1_up[...] = up(rows).astype(BF16)
    ez1[:, :sub] = rows.astype(BF16)
    rows = from_first[:, sub:] + from_second[:, :sub]
    ez1[:, sub : 2 * sub] = (rows * slope1_ref[:, sub : 2 * sub].astype(F32)).astype(BF16)
    rows = from_second[:, sub : 2 * sub]
    ez1[:, 2 * sub : 3 * sub] = (rows * slope1_ref[:, 2 * sub : 3 * sub].astype(F32)).astype(BF16)
    rows = from_second[:, 2 * sub :] + dot_nt(ez2_up_ref[...], two_ref[:sub, :])
    ez1[:, 3 * sub :] = (rows * slope1_ref[:, 3 * sub :].astype(F32)).astype(BF16)
    later = dot_tn(a1_ref[:, sub:], second)
    two_out[:sub, :] = (later[:sub] + dot_tn(a1_ref[:, 3 * sub :], ez2_up_ref[...])).astype(BF16)
    two_out[sub:, :] = (later[sub:] + dot_tn(a1_ref[:, : 2 * sub], first)).astype(BF16)
    wide[...] = dot_tn(mel_ref[...], ez1[...])
    back = dot_tn(mel_ref[:, fold - 128 :], ez1_up[...])[128 - mels :]
    for part in range(3):
        total = back if part == 0 else wide[(part - 1) * mels : part * mels, :sub]
        for j in range(1, 4):
            start = (2 * j - 1 + part) * mels
            total = total + wide[start : start + mels, j * sub : (j + 1) * sub]
        one_out[part * mels : (part + 1) * mels, :] = total.astype(BF16)


def partner(axis, bit):
    count = lax.axis_size(axis)
    return [(i, i ^ (1 << bit)) for i in range(count)]


def bit_of(axis, bit):
    return (lax.axis_index(axis) >> bit) & 1


def halve(rows, axis, bit):
    half = rows.shape[0] // 2
    mine = bit_of(axis, bit)
    sent = lax.dynamic_slice_in_dim(rows, (1 - mine) * half, half, 0)
    kept = lax.dynamic_slice_in_dim(rows, mine * half, half, 0)
    got = lax.ppermute(sent, axis, partner(axis, bit))
    return (kept.astype(F32) + got.astype(F32)).astype(BF16)


def double(rows, axis, bit):
    got = lax.ppermute(rows, axis, partner(axis, bit))
    return (rows.astype(F32) + got.astype(F32)).astype(BF16)


def join(rows, axis, bit):
    got = lax.ppermute(rows, axis, partner(axis, bit))
    first = bit_of(axis, bit) == 0
    return jnp.concatenate([jnp.where(first, rows, got), jnp.where(first, got, rows)], axis=0)


def chain(rows, stages, last):
    for axis, bit in stages:
        rows = halve(rows, axis, bit)
    rows = double(rows, *last)
    for axis, bit in reversed(stages):
        rows = join(rows, axis, bit)
    return rows


def total_sum(rows):
    dp_bits = lax.axis_size("dp").bit_length() - 1
    tm_bits = lax.axis_size("tm").bit_length() - 1
    near = [("tm", b) for b in range(tm_bits)]
    for stage in near:
        rows = halve(rows, *stage)
    far = [("dp", b) for b in range(dp_bits - 1)]
    last = ("dp", dp_bits - 1)
    half = rows.shape[0] // 2
    one = chain(rows[:half], far, last)
    swapped = [far[1], far[0]] + far[2:]
    two = chain(rows[half:], swapped, last)
    rows = jnp.concatenate([one, two], axis=0)
    for stage in reversed(near):
        rows = join(rows, *stage)
    return rows


def per_device(
    mel,
    cotangent,
    conv_one,
    conv_two,
    conv_three,
    linear_weight,
    ln_gain,
    ln_bias,
    proj,
    dw_kernel,
    blocks,
):
    dp_count = lax.axis_size("dp")
    tm_count = lax.axis_size("tm")
    dp_rank = lax.axis_index("dp")
    mel = mel[0]
    cot = cotangent[0]
    rows_dev, fold = mel.shape
    mels = conv_one.shape[0] // 3
    sub = conv_one.shape[1]
    width = linear_weight.shape[1]
    taps = dw_kernel.shape[0]
    half = taps // 2
    block_rows = rows_dev // dp_count
    total_blocks = (dp_count * dp_count + 2) // 3
    live_rows = blocks[dp_rank] * block_rows
    scale = 1.0 / math.sqrt(total_blocks * block_rows * tm_count)
    tm_rank = lax.axis_index("tm")
    rows = rows_dev + PAD
    stride = rows // 8

    pieces = [proj]
    for k in range(1, tm_count):
        pieces.append(
            lax.ppermute(proj, "tm", [(i, (i + k) % tm_count) for i in range(tm_count)])
        )
    order = jnp.mod(tm_rank - jnp.arange(tm_count), tm_count)
    pieces = jnp.stack(pieces)[order]

    tail = jnp.concatenate([cot, mel], axis=1)
    tail = lax.dynamic_slice_in_dim(tail, live_rows - half, half, 0)
    to_right = [(i, i + 1) for i in range(tm_count - 1)]
    to_left = [(i + 1, i) for i in range(tm_count - 1)]
    left = lax.ppermute(tail, "tm", to_right)
    right = lax.ppermute(jnp.concatenate([cot[:half], mel[:half]], axis=1), "tm", to_left)
    halo = jnp.concatenate([right, jnp.zeros((16 - 2 * half, width + fold), BF16), left], axis=0)
    live = live_rows.reshape(1)

    def call(body, inputs, outputs, scratch):
        return pl.pallas_call(
            body,
            out_shape=[jax.ShapeDtypeStruct(shape, dtype) for shape, dtype in outputs],
            in_specs=[
                pl.BlockSpec(memory_space=pltpu.SMEM if x.dtype == jnp.int32 else pltpu.VMEM)
                for x in inputs
            ],
            out_specs=[pl.BlockSpec(memory_space=pltpu.VMEM) for _ in outputs],
            scratch_shapes=[pltpu.VMEM(shape, dtype) for shape, dtype in scratch],
            compiler_params=pltpu.CompilerParams(vmem_limit_bytes=VMEM_BYTES),
        )(*inputs)

    gain = ln_gain[None]
    mel_rows, cot_taps, a1, slope1, a2, slope2, a3, slope3, hidden, shifted = call(
        front,
        [
            live,
            mel,
            cot,
            halo,
            conv_one,
            conv_two,
            conv_three,
            linear_weight,
            gain,
            ln_bias[None],
        ],
        [
            ((rows, fold), BF16),
            ((rows + 8 * (taps - 1), width), BF16),
            ((rows, 4 * sub), BF16),
            ((rows, 4 * sub), BF16),
            ((rows, 2 * sub), BF16),
            ((rows, 2 * sub), BF16),
            ((rows, sub), BF16),
            ((rows, sub), BF16),
            ((rows, width), BF16),
            ((rows, width), BF16),
        ],
        [((fold, 4 * sub), BF16), ((rows, 4 * sub), F32), ((128, sub), BF16)],
    )
    grad_lin, grad_three, small, ez2, ez2_up = call(
        functools.partial(middle, scale=scale),
        [
            live,
            shifted,
            hidden,
            cot_taps,
            pieces,
            dw_kernel,
            gain,
            linear_weight,
            conv_three,
            a3,
            slope3,
            a2,
            slope2,
        ],
        [
            ((sub * (width // LANES), LANES), BF16),
            ((3 * sub, LANES), BF16),
            ((16 * (width // LANES), LANES), BF16),
            ((rows, 2 * sub), BF16),
            ((rows, sub), BF16),
        ],
        [
            ((rows, width), F32),
            ((rows, width), F32),
            ((rows, 2 * width), BF16),
            ((rows, width), BF16),
            ((16, width), F32),
        ],
    )
    grad_two, grad_one = call(
        rear,
        [mel_rows, a1, slope1, ez2, ez2_up, conv_two],
        [((3 * sub, LANES), BF16), ((3 * mels, LANES), BF16)],
        [((rows, 4 * sub), BF16), ((rows, sub), BF16), ((fold, 4 * sub), F32)],
    )

    flat = jnp.concatenate([grad_lin, grad_three, small, grad_two, grad_one], axis=0)
    unit = 8 * dp_count * tm_count
    size = -(-flat.shape[0] // unit) * unit
    summed = total_sum(jnp.pad(flat, ((0, size - flat.shape[0]), (0, 0))))
    results = []
    offset = 0
    for count, blocks_of in (
        (sub, width // LANES),
        (3 * sub, 1),
        (16, width // LANES),
        (3 * sub, 1),
        (3 * mels, 1),
    ):
        piece = summed[offset : offset + count * blocks_of]
        offset += count * blocks_of
        results.append(
            jnp.concatenate([piece[c * count : (c + 1) * count] for c in range(blocks_of)], axis=1)
        )
    out_lin, out_three, out_small, out_two, out_one = results
    return (
        out_one,
        out_two,
        out_three,
        out_lin,
        out_small[0],
        out_small[1],
        out_small[2 : 2 + taps],
    )


def solution(mesh):
    return jax.shard_map(
        per_device,
        mesh=mesh,
        in_specs=(
            P("dp", "tm", None),
            P("dp", "tm", None),
            P(),
            P(),
            P(),
            P(),
            P(),
            P(),
            P(None, "tm"),
            P(),
            P(),
        ),
        out_specs=(P(), P(), P(), P(), P(), P(), P()),
        check_vma=False,
    )
```
